128 devices in a mesh: mem: 8 (over y_hi, z), space: 16 (over y_lo, x, core).
Axes of the slice: x: 4, y: 4 (y_hi: 2, y_lo: 2; y = y_hi * 2 + y_lo), z: 4, core: 2. Of those that a mesh axis runs over, the one named last changes fastest.
Arguments:
- theta: float32 [256, 64, 64, 128], P('mem', 'space'), may hold values from -1 to 1
- start: float32 [64, 64, 128], P('space'), may hold values from -6 to 6
- sensors: int32 [4096], replicated, may hold values from 0 to 4095
- observed: float32 [4096], P('space'), may hold values from -6 to 6
- noise: float32 [4096, 256], P('space', 'mem'), may hold values from -3 to 3
- variance: float32 [4096], P('space'), may hold values from 0.25 to 4
Outputs:
- updated: float32 [256, 64, 64, 128], P('mem', 'space')
- predicted: float32 [4096, 256], P('space', 'mem')
The draws below stay inside these ranges and needn't reach their ends.
All inputs are finite; a program needn't handle non-finite values.
Results may differ from the reference program's by a relative error of at most 0.0085.
Values may be sent and summed in bfloat16 or wider, within the bound.
No kernel may reach another device: no remote copies, remote signals or barrier semaphores. Data moves between devices by JAX's collectives and lax.ppermute only.
A program may use at most 192 MiB of HBM per device.

```python
import math
import jax
import jax.numpy as jnp
from jax import lax

NX = 64
NY = 128
SENS = 4096
STEPS = 3
M = 256
NZ = 64


def plant(drawn, rng, low, largest):
    spot = [jax.random.randint(jax.random.fold_in(rng, axis), (), 0, length) for axis, length in enumerate(drawn.shape)]
    widest = drawn.shape.index(max(drawn.shape))
    next_to = spot[:widest] + [(spot[widest] + 1) % drawn.shape[widest]] + spot[widest + 1:]
    return drawn.at[tuple(spot)].set(low).at[tuple(next_to)].set(largest)


def shard_levels(rng, shape, split, least, top_value):
    level, own = 1.0, jax.random.fold_in(rng, 6)
    for axis_at, shards_of in split:
        draws = jnp.exp(jax.random.uniform(jax.random.fold_in(own, axis_at), (shards_of,), jnp.float32, least / len(split), top_value / len(split)))
        level = level * jnp.repeat(draws, shape[axis_at] // shards_of).reshape([-1 if axis == axis_at else 1 for axis in range(len(shape))])
    return level


def centred(stream_key, shape, scale, reach, shards=(), held_as=jnp.bfloat16):
    loudness = shard_levels(stream_key, shape, shards, -0.22, 0.18) if shards else 1.0
    values = jax.random.normal(stream_key, shape, jnp.float32) * scale * loudness
    return jnp.minimum(jnp.maximum(values, -reach), reach).astype(held_as)


def setup_inputs(seed: int = 0) -> dict:
    key_of = jax.random.split(jax.random.key(seed), 7)
    theta = jnp.clip(jax.random.uniform(key_of[0], (M, NZ, NX, NY), jnp.float32, -1.0, 1.0) * shard_levels(key_of[0], (M, NZ, NX, NY), ((0, 8), (1, 16)), -0.4, 0.0), -1.0, 1.0)
    start = centred(key_of[1], (NZ, NX, NY), 1.0, 6.0, ((0, 16),), jnp.float32)
    sensors = plant(jax.random.randint(key_of[2], (SENS,), 0, NZ * NX), jax.random.fold_in(key_of[2], 1), 0, (NZ * NX) - 1).astype(jnp.int32)
    observed = centred(key_of[3], (SENS,), 1.0, 6.0, ((0, 16),), jnp.float32)
    noise = centred(key_of[4], (SENS, M), 0.5, 3.0, ((0, 16), (1, 8)), jnp.float32)
    variance = jnp.clip(jnp.exp(math.log(4.0) - 2.7725887 * jax.random.uniform(key_of[5], (SENS,), jnp.float32) ** shard_levels(key_of[5], (SENS,), ((0, 16),), -0.2, 0.2)), 0.25, 4.0)
    return {"theta": theta, "start": start, "sensors": sensors, "observed": observed, "noise": noise, "variance": variance}


step_size = 0.055

def harmonic(left_k, right_k):
    return 2.0 * left_k * right_k / (left_k + right_k)

def face_terms(padded):
    inner_k = padded[:, 1:-1]
    side_pad = jnp.pad(inner_k, ((0, 0), (0, 0), (1, 1), (1, 1)), constant_values=1.0)
    return (harmonic(inner_k, padded[:, :-2]), harmonic(inner_k, padded[:, 2:]), harmonic(inner_k, side_pad[:, :, :-2, 1:-1]), harmonic(inner_k, side_pad[:, :, 2:, 1:-1]), harmonic(inner_k, side_pad[:, :, 1:-1, :-2]), harmonic(inner_k, side_pad[:, :, 1:-1, 2:]))

def advance(padded, face_coef):
    field_now = padded[:, 1:-1]
    side_pad = jnp.pad(field_now, ((0, 0), (0, 0), (1, 1), (1, 1)))
    net_flux = face_coef[0] * (padded[:, :-2] - field_now) + face_coef[1] * (padded[:, 2:] - field_now)
    net_flux = net_flux + face_coef[2] * (side_pad[:, :, :-2, 1:-1] - field_now) + face_coef[3] * (side_pad[:, :, 2:, 1:-1] - field_now)
    net_flux = net_flux + face_coef[4] * (side_pad[:, :, 1:-1, :-2] - field_now) + face_coef[5] * (side_pad[:, :, 1:-1, 2:] - field_now)
    return field_now + step_size * net_flux

def reference(theta, start, sensors, observed, noise, variance):

    def evolve(theta_one):
        conduct = jnp.exp(theta_one)[None]
        padded = jnp.pad(conduct, ((0, 0), (1, 1), (0, 0), (0, 0)), constant_values=1.0)
        face_coef = face_terms(padded)
        field_now = start[None]
        for step_index in range(STEPS):
            field_now = advance(jnp.pad(field_now, ((0, 0), (1, 1), (0, 0), (0, 0))), face_coef)
        line_sums = lax.optimization_barrier(jnp.sum(field_now[0], axis=2)).reshape(-1)
        return line_sums[sensors] / math.sqrt(NY)
    predicted = lax.map(evolve, theta).T
    center = lax.optimization_barrier(jnp.mean(predicted, axis=1, keepdims=True))
    weight = (1.0 / jnp.sqrt(variance))[:, None]
    spread = (predicted - center) * weight / math.sqrt(M - 1)
    misfit = (observed[:, None] + noise - predicted) * weight
    gram_part = jnp.dot(spread.T, spread, precision=lax.Precision.HIGHEST)
    right_part = jnp.dot(spread.T, misfit, precision=lax.Precision.HIGHEST)
    system = gram_part + jnp.eye(M, dtype=jnp.float32)
    factor = jnp.linalg.cholesky(system)
    mixing = jax.scipy.linalg.cho_solve((factor, True), right_part)
    mixing_low = mixing.astype(jnp.bfloat16)
    fields = theta.astype(jnp.bfloat16).reshape(M, -1)
    combined = lax.dot_general(mixing_low.astype(jnp.float32), fields.astype(jnp.float32), (((0,), (0,)), ((), ())), preferred_element_type=jnp.float32)
    updated = theta + (combined / math.sqrt(M - 1)).reshape(theta.shape)
    return (updated, predicted)
```

```python
import functools
import math

import jax
import jax.numpy as jnp
from jax import lax
from jax.experimental import pallas as pl
from jax.experimental.pallas import tpu as pltpu
from jax.sharding import PartitionSpec as P

STEPS = 3
STEP_SIZE = 0.055
OUTSIDE = 1.0 / (2.0 * STEP_SIZE)
HIGH = lax.Precision.HIGHEST
NT = (((1,), (1,)), ((), ()))
MIB = 1 << 20


def inverse(x):
    guess = pl.reciprocal(x, approx=True)
    return guess * (2.0 - x * guess)


def diffuse_kernel(edge_ref, theta_ref, low_ref, high_ref, start_ref, out_ref, cx, cy, cz, keep, u1, u2, u3):
    members, planes, rows, lanes = theta_ref.shape
    width = low_ref.shape[1]
    total = planes + 2 * width
    row_at = lax.broadcasted_iota(jnp.int32, (rows, lanes), 0)
    lane_at = lax.broadcasted_iota(jnp.int32, (rows, lanes), 1)
    last_row, last_lane = row_at == rows - 1, lane_at == lanes - 1
    sides = (
        (row_at == 0).astype(jnp.float32)
        + last_row.astype(jnp.float32)
        + (lane_at == 0).astype(jnp.float32)
        + last_lane.astype(jnp.float32)
    )
    low_edge, high_edge = edge_ref[0], edge_ref[1]

    def up(v, axis):
        return pltpu.roll(v, v.shape[axis] - 1, axis)

    def down(v, axis):
        return pltpu.roll(v, 1, axis)

    @pl.loop(0, members)
    def _(m):
        def resistance(p):
            if p < width:
                t = low_ref[m, p].astype(jnp.float32)
            elif p < width + planes:
                t = theta_ref[m, p - width]
            else:
                t = high_ref[m, p - width - planes].astype(jnp.float32)
            return jnp.exp(math.log(OUTSIDE) - t)

        fields = [start_ref, u1, u2, u3]
        flux_z = [None] * STEPS

        def advance(step, p):
            source = fields[step]
            u = source[p]
            if flux_z[step] is None:
                flux_z[step] = cz[p - 1] * (u - source[p - 1])
            fx = cx[p] * (up(u, 0) - u)
            fy = cy[p] * (up(u, 1) - u)
            fz = cz[p] * (source[p + 1] - u)
            new = keep[p] * u + ((fx - down(fx, 0)) + (fy - down(fy, 1)) + (fz - flux_z[step]))
            flux_z[step] = fz
            if p < width:
                new = new * low_edge
            elif p >= width + planes:
                new = new * high_edge
            if step == STEPS - 1:
                u3[p - width] = new
            else:
                fields[step + 1][p] = new

        before = None
        for p in range(total):
            r = resistance(p)
            if before is not None:
                cz[p - 1] = inverse(before + r)
            before = r
            if 1 <= p < total - 1:
                cx[p] = jnp.where(last_row, 0.0, inverse(r + up(r, 0)))
                cy[p] = jnp.where(last_lane, 0.0, inverse(r + up(r, 1)))
                keep[p] = 1.0 - sides * inverse(r + OUTSIDE)
            for step in range(STEPS):
                q = p - 1 - step
                if step + 1 <= q < total - 1 - step:
                    advance(step, q)
        ones = jnp.ones((8, lanes), jnp.float32)
        sums = lax.dot_general(
            ones, u3[...].reshape(planes * rows, lanes), NT, precision=HIGH, preferred_element_type=jnp.float32
        )
        out_ref[pl.ds(m, 1), :] = sums[0:1]


def diffuse(theta, low, high, start_ext, edges):
    members, planes, rows, lanes = theta.shape
    width = low.shape[1]
    total = planes + 2 * width
    some = 8
    shape = (total, rows, lanes)
    return pl.pallas_call(
        diffuse_kernel,
        grid=(members // some,),
        in_specs=[
            pl.BlockSpec(memory_space=pltpu.SMEM),
            pl.BlockSpec((some, planes, rows, lanes), lambda i: (i, 0, 0, 0)),
            pl.BlockSpec((some, width, rows, lanes), lambda i: (i, 0, 0, 0)),
            pl.BlockSpec((some, width, rows, lanes), lambda i: (i, 0, 0, 0)),
            pl.BlockSpec(shape, lambda i: (0, 0, 0)),
        ],
        out_specs=pl.BlockSpec((some, planes * rows), lambda i: (i, 0)),
        out_shape=jax.ShapeDtypeStruct((members, planes * rows), jnp.float32),
        scratch_shapes=[pltpu.VMEM(shape, jnp.float32)] * 6 + [pltpu.VMEM((planes, rows, lanes), jnp.float32)],
        compiler_params=pltpu.CompilerParams(vmem_limit_bytes=24 * MIB),
        cost_estimate=pl.CostEstimate(flops=300 * theta.size, bytes_accessed=8 * theta.size, transcendentals=12 * theta.size),
        name="diffuse",
    )(edges, theta, low, high, start_ext)


def gram_kernel(scale, lines_ref, own_ref, data_ref, out_ref):
    everyone, count = lines_ref.shape
    members = own_ref.shape[0]
    value = lines_ref[...] * scale
    dev = value - jnp.mean(value, axis=0, keepdims=True)
    weight = data_ref[members : members + 1, :]
    left = jnp.concatenate(
        [
            dev * (weight * (1.0 / (everyone - 1))),
            (data_ref[0:members, :] - weight * (own_ref[...] * scale)) * (1.0 / math.sqrt(everyone - 1)),
        ],
        axis=0,
    )
    both = lax.dot_general(left, dev, NT, precision=HIGH, preferred_element_type=jnp.float32)
    chunks, depth, _ = out_ref.shape
    a, b = everyone // chunks, members // chunks
    pad = jnp.zeros((depth - a - b, everyone), jnp.float32)
    for c in range(chunks):
        out_ref[c, 0:a] = both[a * c : a * (c + 1)]
        out_ref[c, a : a + b] = both[everyone + b * c : everyone + b * (c + 1)]
        out_ref[c, a + b :] = pad


def invert_block(block):
    size = block.shape[0]
    lane_at = lax.broadcasted_iota(jnp.int32, (1, size), 1)
    row_at = lax.broadcasted_iota(jnp.int32, (8, 1), 0)
    groups = [block[8 * g : 8 * g + 8] for g in range(size // 8)]
    for k in range(size):
        g, s = divmod(k, 8)
        here = lane_at == k
        pivot_row = groups[g][s : s + 1]
        d = 1.0 / pivot_row[:, k : k + 1]
        row = jnp.where(here, d, pivot_row * d)
        new = []
        for i, rows in enumerate(groups):
            col = rows[:, k : k + 1]
            next_rows = jnp.where(here, 0.0, rows) - col * row
            if i == g:
                next_rows = jnp.where(row_at == s, row, next_rows)
            new.append(next_rows)
        groups = new
    return jnp.concatenate(groups, axis=0)


def solve_kernel(parts_ref, target_ref, out_ref, work, inv):
    chunks, depth, size = parts_ref.shape
    a = size // chunks
    b = depth_rows = out_ref.shape[0] // chunks
    half = size // 2
    rhs = []
    for c in range(chunks):
        work[a * c : a * (c + 1)] = parts_ref[c, 0:a]
        rhs.append(parts_ref[c, a : a + b])
    rhs = jnp.concatenate(rhs, axis=0)
    eye = (
        lax.broadcasted_iota(jnp.int32, (half, half), 0) == lax.broadcasted_iota(jnp.int32, (half, half), 1)
    ).astype(jnp.float32)
    work[0:half, 0:half] += eye
    work[half:, half:] += eye
    dot = functools.partial(jnp.dot, precision=HIGH, preferred_element_type=jnp.float32)

    @pl.loop(0, 2)
    def _(i):
        at = pl.ds(pl.multiple_of(i * half, half), half)

        @pl.when(i == 1)
        def _():
            cross = dot(work[half:, 0:half], inv[0])
            work[half:, half:] = work[half:, half:] - dot(cross, work[0:half, half:])

        inv[i] = invert_block(work[at, at])

    cross = dot(work[half:, 0:half], inv[0])
    first = dot(rhs[:, 0:half], inv[0])
    second = dot(rhs[:, half:] - dot(first, work[0:half, half:]), inv[1])
    first = first - dot(second, cross)
    mixing = jnp.concatenate([first, second], axis=1).astype(jnp.bfloat16)
    order = (lax.broadcasted_iota(jnp.int32, (size, size), 0) == target_ref[...]).astype(jnp.float32).astype(jnp.bfloat16)
    out_ref[...] = jnp.dot(mixing, order, preferred_element_type=jnp.float32).astype(jnp.bfloat16)


def combine_kernel(scale, mix_ref, theta_ref, *refs):
    blocks, out_ref = refs[:-1], refs[-1]
    everyone = jnp.concatenate([ref[...] for ref in blocks], axis=0)
    result = jnp.dot(mix_ref[...], everyone, preferred_element_type=jnp.float32) * scale
    members, rows, lanes = theta_ref.shape
    for r in range(rows):
        out_ref[:, r, :] = theta_ref[:, r, :] + result[:, r * lanes : (r + 1) * lanes]


def combine(mix, theta, blocks):
    members, planes, rows, lanes = theta.shape
    flat = theta.reshape(members, planes * rows, lanes)
    everyone = sum(block.shape[0] for block in blocks)
    some = 16
    out = pl.pallas_call(
        functools.partial(combine_kernel, 1.0 / math.sqrt(everyone - 1)),
        grid=(planes * rows // some,),
        in_specs=[
            pl.BlockSpec(mix.shape, lambda i: (0, 0)),
            pl.BlockSpec((members, some, lanes), lambda i: (0, i, 0)),
        ]
        + [pl.BlockSpec((block.shape[0], some * lanes), lambda i: (0, i)) for block in blocks],
        out_specs=pl.BlockSpec((members, some, lanes), lambda i: (0, i, 0)),
        out_shape=jax.ShapeDtypeStruct(flat.shape, jnp.float32),
        compiler_params=pltpu.CompilerParams(vmem_limit_bytes=24 * MIB),
        cost_estimate=pl.CostEstimate(flops=2 * everyone * theta.size, bytes_accessed=24 * theta.size // 1, transcendentals=0),
        name="combine",
    )(mix, flat, *blocks)
    return out.reshape(theta.shape)


def spread_out(block, axis):
    count = lax.axis_size(axis)
    return lax.all_to_all(jnp.broadcast_to(block[None], (count,) + block.shape), axis, 0, 0)


def body(theta, start, sensors, observed, noise, variance):
    members, planes, rows, lanes = theta.shape
    spaces, mems = lax.axis_size("space"), lax.axis_size("mem")
    lines_here = planes * rows
    mine, me = lax.axis_index("space"), lax.axis_index("mem")
    width = STEPS
    low_theta = theta.astype(jnp.bfloat16)
    forward = [(i, i + 1) for i in range(spaces - 1)]
    backward = [(i + 1, i) for i in range(spaces - 1)]
    theta_low = lax.ppermute(low_theta[:, planes - width :], "space", forward)
    theta_high = lax.ppermute(low_theta[:, :width], "space", backward)
    start_low = lax.ppermute(start[planes - width :], "space", forward)
    start_high = lax.ppermute(start[:width], "space", backward)
    start_ext = jnp.concatenate([start_low, start, start_high], axis=0)
    edges = jnp.stack([mine > 0, mine < spaces - 1]).astype(jnp.float32)

    ring = mems // 2
    along = lambda k: [(i, (i // ring) * ring + (i + k) % ring) for i in range(mems)]
    across = [(i, (i + ring) % mems) for i in range(mems)]
    own = low_theta.reshape(members, lines_here * lanes)
    z_low = lax.ppermute(own, "mem", along(1))
    z_high = lax.ppermute(own, "mem", along(ring - 1))
    theta_low, theta_high, start_ext, own_y = lax.optimization_barrier((theta_low, theta_high, start_ext, own))
    y_own = lax.ppermute(own_y, "mem", across)

    line_at = jnp.arange(spaces * lines_here, dtype=jnp.int32)
    rows_here = observed.shape[0]
    sensors_here = lax.dynamic_slice_in_dim(sensors, mine * rows_here, rows_here, 0)
    pick = (sensors_here[:, None] == line_at[None, :]).astype(jnp.float32)
    inv_var = 1.0 / variance
    data = jnp.concatenate([(observed[None, :] + noise.T) * inv_var[None, :], inv_var[None, :]], axis=0)
    data = jnp.pad(data, ((0, 7), (0, 0)))
    by_line = jnp.dot(data, pick, precision=HIGH).reshape(members + 8, spaces, lines_here).transpose(1, 0, 2)
    by_line = jnp.sum(lax.all_to_all(by_line, "space", 0, 0), axis=0)

    lines = diffuse(theta, theta_low, theta_high, start_ext, edges)
    everyone = members * mems
    lines_all = spread_out(lines, "mem").reshape(everyone, lines_here)
    scale = 1.0 / math.sqrt(lanes)
    depth = 24
    partial_sums = pl.pallas_call(
        functools.partial(gram_kernel, scale),
        out_shape=jax.ShapeDtypeStruct((spaces, depth, everyone), jnp.float32),
        compiler_params=pltpu.CompilerParams(vmem_limit_bytes=16 * MIB),
        name="gram",
    )(lines_all, lines, by_line)
    sums = jnp.sum(lax.all_to_all(partial_sums, "space", 0, 0), axis=0)
    whole = spread_out(sums, "space")

    half = members // 2
    z_low, z_high, _ = lax.optimization_barrier((z_low, z_high, lines))
    far_a = lax.ppermute(z_low[:half], "mem", along(1))
    far_b = lax.ppermute(z_high[half:], "mem", along(ring - 1))
    y_low = lax.ppermute(y_own, "mem", along(1))
    y_high = lax.ppermute(y_own, "mem", along(ring - 1))
    y_far_a = lax.ppermute(far_a, "mem", across)
    y_far_b = lax.ppermute(far_b, "mem", across)

    lines_slabs = spread_out(lines, "space")
    lines_slabs = lines_slabs.transpose(1, 0, 2).reshape(members, spaces * lines_here)
    predicted = (jnp.dot(lines_slabs, pick.T, precision=HIGH) * scale).T

    steps = jnp.array([0, ring - 1, 1, 2], jnp.int32)
    row_y, row_z = me // ring, me % ring
    blocks_at = jnp.concatenate(
        [(row_y ^ side) * ring + (row_z + steps) % ring for side in (0, 1)]
    )
    target = (blocks_at[:, None] * members + jnp.arange(members, dtype=jnp.int32)[None, :]).reshape(1, everyone)
    mix = pl.pallas_call(
        solve_kernel,
        out_shape=jax.ShapeDtypeStruct((members, everyone), jnp.bfloat16),
        scratch_shapes=[
            pltpu.VMEM((everyone, everyone), jnp.float32),
            pltpu.VMEM((2, everyone // 2, everyone // 2), jnp.float32),
        ],
        compiler_params=pltpu.CompilerParams(vmem_limit_bytes=16 * MIB),
        name="solve",
    )(whole, target)
    updated = combine(mix, theta, [own, z_low, z_high, far_a, far_b, y_own, y_low, y_high, y_far_a, y_far_b])
    return (updated, predicted)


def solution(mesh):
    in_specs = (
        P("mem", "space", None, None),
        P("space", None, None),
        P(),
        P("space"),
        P("space", "mem"),
        P("space"),
    )
    out_specs = (P("mem", "space", None, None), P("space", "mem"))
    return jax.shard_map(body, mesh=mesh, in_specs=in_specs, out_specs=out_specs, check_vma=False)
```

```python
import functools
import math

import jax
import jax.numpy as jnp
from jax import lax
from jax.experimental import pallas as pl
from jax.experimental.pallas import tpu as pltpu
from jax.sharding import PartitionSpec as P

STEPS = 3
STEP_SIZE = 0.055
OUTSIDE = 1.0 / (2.0 * STEP_SIZE)
HIGH = lax.Precision.HIGHEST
NT = (((1,), (1,)), ((), ()))
MIB = 1 << 20
PIVOTS = 8


def inverse(x):
    return pl.reciprocal(x, approx=True)


def diffuse_kernel(
    edge_ref, theta_ref, low_ref, high_ref, low_start_ref, high_start_ref, own_start_ref,
    out_ref, cx, cy, cz, keep, u0, u1, u2, u3,
):
    members, planes, rows, lanes = theta_ref.shape
    width = low_ref.shape[1]
    total = planes + 2 * width
    row_at = lax.broadcasted_iota(jnp.int32, (rows, lanes), 0)
    lane_at = lax.broadcasted_iota(jnp.int32, (rows, lanes), 1)
    last_row, last_lane = row_at == rows - 1, lane_at == lanes - 1
    sides = (
        (row_at == 0).astype(jnp.float32)
        + last_row.astype(jnp.float32)
        + (lane_at == 0).astype(jnp.float32)
        + last_lane.astype(jnp.float32)
    )
    low_edge, high_edge = edge_ref[0], edge_ref[1]

    @pl.when(pl.program_id(0) == 0)
    def _():
        u0[0:width] = low_start_ref[0].astype(jnp.float32) + low_start_ref[1].astype(jnp.float32)
        u0[width : width + planes] = own_start_ref[...]
        u0[width + planes :] = high_start_ref[0].astype(jnp.float32) + high_start_ref[1].astype(jnp.float32)

    def up(v, axis):
        return pltpu.roll(v, v.shape[axis] - 1, axis)

    def down(v, axis):
        return pltpu.roll(v, 1, axis)

    @pl.loop(0, members)
    def _(m):
        def resistance(p):
            if p < width:
                t = low_ref[m, p].astype(jnp.float32)
            elif p < width + planes:
                t = theta_ref[m, p - width]
            else:
                t = high_ref[m, p - width - planes].astype(jnp.float32)
            return jnp.exp(math.log(OUTSIDE) - t)

        fields = [u0, u1, u2, u3]
        flux_z = [None] * STEPS

        def advance(step, p):
            source = fields[step]
            u = source[p]
            if flux_z[step] is None:
                flux_z[step] = cz[p - 1] * (u - source[p - 1])
            fx = cx[p] * (up(u, 0) - u)
            fy = cy[p] * (up(u, 1) - u)
            fz = cz[p] * (source[p + 1] - u)
            new = keep[p] * u + ((fx - down(fx, 0)) + (fy - down(fy, 1)) + (fz - flux_z[step]))
            flux_z[step] = fz
            if p < width:
                new = new * low_edge
            elif p >= width + planes:
                new = new * high_edge
            if step == STEPS - 1:
                u3[p - width] = new
            else:
                fields[step + 1][p] = new

        before = None
        for p in range(total):
            r = resistance(p)
            if before is not None:
                cz[p - 1] = inverse(before + r)
            before = r
            if 1 <= p < total - 1:
                cx[p] = jnp.where(last_row, 0.0, inverse(r + up(r, 0)))
                cy[p] = jnp.where(last_lane, 0.0, inverse(r + up(r, 1)))
                keep[p] = 1.0 - sides * inverse(r + OUTSIDE)
            for step in range(STEPS):
                q = p - 1 - step
                if step + 1 <= q < total - 1 - step:
                    advance(step, q)
        ones = jnp.ones((8, lanes), jnp.float32)
        sums = lax.dot_general(
            ones, u3[...].reshape(planes * rows, lanes), NT, precision=HIGH, preferred_element_type=jnp.float32
        )
        out_ref[pl.ds(m, 1), :] = sums[0:1]


def diffuse(theta, first, low, high, begin_low, begin_high, start, edges):
    planes, rows, lanes = theta.shape[1:]
    members, width = low.shape[:2]
    members -= members % 8
    total = planes + 2 * width
    some = 8
    skip, last = first // some, begin_low.shape[0] // 2 - 1
    shape = (total, rows, lanes)
    return pl.pallas_call(
        diffuse_kernel,
        grid=(members // some,),
        in_specs=[
            pl.BlockSpec(memory_space=pltpu.SMEM),
            pl.BlockSpec((some, planes, rows, lanes), lambda i: (i + skip, 0, 0, 0)),
            pl.BlockSpec((some, width, rows, lanes), lambda i: (i, 0, 0, 0)),
            pl.BlockSpec((some, width, rows, lanes), lambda i: (i, 0, 0, 0)),
            pl.BlockSpec((2, width, rows, lanes), lambda i: (last, 0, 0, 0)),
            pl.BlockSpec((2, width, rows, lanes), lambda i: (last, 0, 0, 0)),
            pl.BlockSpec((planes, rows, lanes), lambda i: (0, 0, 0)),
        ],
        out_specs=pl.BlockSpec((some, planes * rows), lambda i: (i, 0)),
        out_shape=jax.ShapeDtypeStruct((members, planes * rows), jnp.float32),
        scratch_shapes=[pltpu.VMEM(shape, jnp.float32)] * 7 + [pltpu.VMEM((planes, rows, lanes), jnp.float32)],
        compiler_params=pltpu.CompilerParams(vmem_limit_bytes=50 * MIB),
        cost_estimate=pl.CostEstimate(flops=300 * theta.size, bytes_accessed=50 * theta.size, transcendentals=12 * theta.size),
        name="diffuse",
    )(edges, theta, low, high, begin_low, begin_high, start)


def gram_kernel(scale, lines_ref, data_ref, weight_ref, out_ref):
    everyone, count = lines_ref.shape
    value = lines_ref[...] * scale
    dev = value - jnp.mean(value, axis=0, keepdims=True)
    weight = weight_ref[0:1, :]
    dot = functools.partial(lax.dot_general, dimension_numbers=NT, precision=HIGH, preferred_element_type=jnp.float32)
    gram = dot(dev * (weight * (1.0 / (everyone - 1))), dev)
    right = dot((data_ref[...] - weight * value) * (1.0 / math.sqrt(everyone - 1)), dev)
    chunks = out_ref.shape[0]
    a = everyone // chunks
    for c in range(chunks):
        out_ref[c, 0:a] = gram[a * c : a * (c + 1)]
        out_ref[c, a:] = right[a * c : a * (c + 1)]


def invert_block(block):
    size = block.shape[0]
    lane_at = lax.broadcasted_iota(jnp.int32, (1, size), 1)
    row_at = lax.broadcasted_iota(jnp.int32, (8, 1), 0)
    groups = [block[8 * g : 8 * g + 8] for g in range(size // 8)]
    span = range(PIVOTS)
    for k in range(0, size, PIVOTS):
        g, s = divmod(k, 8)
        here = (lane_at >= k) & (lane_at < k + PIVOTS)
        rows = [groups[g][s + i : s + i + 1] for i in span]
        pivot = [[jnp.broadcast_to(row[:, k + j : k + j + 1], (1, size)) for j in span] for row in rows]
        rows = [jnp.where(here, (lane_at == k + i).astype(jnp.float32), row) for i, row in enumerate(rows)]
        for i in span:
            d = inverse(pivot[i][i])
            rows[i] = rows[i] * d
            for j in range(i + 1, PIVOTS):
                pivot[i][j] = pivot[i][j] * d
            for other in span:
                if other != i:
                    f = pivot[other][i]
                    rows[other] = rows[other] - f * rows[i]
                    for j in range(i + 1, PIVOTS):
                        pivot[other][j] = pivot[other][j] - f * pivot[i][j]
        new = []
        for i, old in enumerate(groups):
            next_rows = jnp.where(here, 0.0, old)
            for j in span:
                next_rows = next_rows - old[:, k + j : k + j + 1] * rows[j]
            if i == g:
                for j in span:
                    next_rows = jnp.where(row_at == s + j, rows[j], next_rows)
            new.append(next_rows)
        groups = new
    return jnp.concatenate(groups, axis=0)


def solve_kernel(parts_ref, out_ref, work, rhs, inv):
    chunks, depth, size = parts_ref.shape
    a = size // chunks
    half = size // 2
    for c in range(chunks):
        work[a * c : a * (c + 1)] = parts_ref[c, 0:a]
        rhs[a * c : a * (c + 1)] = parts_ref[c, a:]
    eye = (
        lax.broadcasted_iota(jnp.int32, (half, half), 0) == lax.broadcasted_iota(jnp.int32, (half, half), 1)
    ).astype(jnp.float32)
    work[0:half, 0:half] += eye
    work[half:, half:] += eye
    dot = functools.partial(jnp.dot, precision=HIGH, preferred_element_type=jnp.float32)

    @pl.loop(0, 2)
    def _(i):
        at = pl.ds(pl.multiple_of(i * half, half), half)

        @pl.when(i == 1)
        def _():
            cross = dot(work[half:, 0:half], inv[0])
            work[half:, half:] = work[half:, half:] - dot(cross, work[0:half, half:])

        inv[i] = invert_block(work[at, at])

    cross = dot(work[half:, 0:half], inv[0])
    first = dot(rhs[:, 0:half], inv[0])
    second = dot(rhs[:, half:] - dot(first, work[0:half, half:]), inv[1])
    out_ref[:, 0:half] = (first - dot(second, cross)).astype(jnp.bfloat16)
    out_ref[:, half:] = second.astype(jnp.bfloat16)


def shared_kernel(scale, mix_ref, fields_ref, out_ref):
    some = 512
    for c in range(0, out_ref.shape[1], some):
        result = jnp.dot(mix_ref[...], fields_ref[:, c : c + some], preferred_element_type=jnp.float32)
        out_ref[:, c : c + some] = (result * scale).astype(jnp.bfloat16)


def finish_kernel(theta_ref, change_ref, out_ref):
    members, some, lanes = theta_ref.shape
    for m in range(0, members, 8):
        change = change_ref[0, m : m + 8, :].astype(jnp.float32)
        change = jnp.stack([change[:, r * lanes : (r + 1) * lanes] for r in range(some)])
        out_ref[m : m + 8] = theta_ref[m : m + 8] + jnp.swapaxes(change, 0, 1)


def finish(theta, changes):
    members, rows, lanes = theta.shape
    chunks, _, cells = changes.shape
    some = cells // lanes
    block = pl.BlockSpec((members, some, lanes), lambda i: (0, i, 0))
    return pl.pallas_call(
        finish_kernel,
        grid=(chunks,),
        in_specs=[block, pl.BlockSpec((1, members, cells), lambda i: (i, 0, 0))],
        out_specs=block,
        out_shape=jax.ShapeDtypeStruct(theta.shape, jnp.float32),
        compiler_params=pltpu.CompilerParams(vmem_limit_bytes=50 * MIB),
        cost_estimate=pl.CostEstimate(flops=2 * changes.size, bytes_accessed=10 * changes.size, transcendentals=0),
        name="finish",
    )(theta, changes)


def after(block, *others):
    return lax.optimization_barrier((block,) + others)[0]


def spread_out(block, axis):
    count = lax.axis_size(axis)
    return lax.all_to_all(jnp.broadcast_to(block[None], (count,) + block.shape), axis, 0, 0)


def after(block, *others):
    return lax.optimization_barrier((block,) + others)[0]


def body(theta, start, sensors, observed, noise, variance):
    members, planes, rows, lanes = theta.shape
    spaces, mems = lax.axis_size("space"), lax.axis_size("mem")
    lines_here = planes * rows
    everyone = members * mems
    mine, me = lax.axis_index("space"), lax.axis_index("mem")
    width = STEPS
    scale = 1.0 / math.sqrt(lanes)
    line_at = jnp.arange(spaces * lines_here, dtype=jnp.int32)
    rows_here = observed.shape[0]
    sensors_here = lax.dynamic_slice_in_dim(sensors, mine * rows_here, rows_here, 0)
    pick = (sensors_here[:, None] == line_at[None, :]).astype(jnp.float32)
    inv_var = 1.0 / variance
    data = jnp.concatenate([(observed[None, :] + noise.T) * inv_var[None, :], inv_var[None, :]], axis=0)
    data = jnp.pad(data, ((0, 7), (0, 0)))
    by_line = jnp.dot(data, pick, precision=HIGH).reshape(members + 8, spaces, lines_here).transpose(1, 0, 2)
    by_line = lax.all_to_all(by_line, "space", 0, 0)
    low_theta = theta.astype(jnp.bfloat16)
    coarse = lax.reduce_precision(start, 8, 7)
    fine = (start - coarse).astype(jnp.bfloat16)
    begin = jnp.stack([coarse.astype(jnp.bfloat16), fine])
    forward = [(i, i + 1) for i in range(spaces - 1)]
    backward = [(i + 1, i) for i in range(spaces - 1)]
    half = members // 2
    top, bottom = slice(planes - width, planes), slice(0, width)
    to_high = jnp.concatenate([low_theta[:half, top], begin[:, top]], axis=0)
    to_low = jnp.concatenate([low_theta[:half, bottom], begin[:, bottom]], axis=0)
    to_high_b, to_low_b = low_theta[half:, top], low_theta[half:, bottom]
    share_rows = lines_here // mems
    shares = low_theta.reshape(members, mems, share_rows, lanes).transpose(1, 0, 2, 3)
    shares = after(shares, by_line, to_high, to_low, to_high_b, to_low_b)
    halo_low = lax.ppermute(to_high, "space", forward)
    halo_high = lax.ppermute(to_low, "space", backward)
    halo_low_b = lax.ppermute(to_high_b, "space", forward)
    halo_high_b = lax.ppermute(to_low_b, "space", backward)
    edges = jnp.stack([mine > 0, mine < spaces - 1]).astype(jnp.float32)

    shared = lax.all_to_all(shares, "mem", 0, 0)
    cells = share_rows * lanes

    lines_a = diffuse(theta, 0, halo_low, halo_high, halo_low, halo_high, start, edges)
    lines_b = diffuse(theta, half, halo_low_b, halo_high_b, halo_low, halo_high, start, after(edges, lines_a))
    lines = jnp.concatenate([lines_a, lines_b], axis=0)
    lines, shared = lax.optimization_barrier((lines, shared))
    by_line = jnp.sum(by_line, axis=0)
    weights = by_line[members:]
    both = spread_out(jnp.stack([lines, by_line[:members]]), "mem")
    both, shared = lax.optimization_barrier((both, shared.reshape(everyone, cells)))
    lines_all = both[:, 0].reshape(everyone, lines_here)
    data_all = both[:, 1].reshape(everyone, lines_here)
    partial_sums = pl.pallas_call(
        functools.partial(gram_kernel, scale),
        out_shape=jax.ShapeDtypeStruct((spaces, 2 * everyone // spaces, everyone), jnp.float32),
        compiler_params=pltpu.CompilerParams(vmem_limit_bytes=50 * MIB),
        name="gram",
    )(lines_all, data_all, weights)
    sums = jnp.sum(lax.all_to_all(partial_sums, "space", 0, 0), axis=0)
    whole = spread_out(sums, "space")

    lines_slabs = spread_out(after(lines, whole), "space")
    lines_slabs = lines_slabs.transpose(1, 0, 2).reshape(members, spaces * lines_here)
    predicted = (jnp.dot(lines_slabs, pick.T, precision=HIGH) * scale).T

    mix = pl.pallas_call(
        solve_kernel,
        out_shape=jax.ShapeDtypeStruct((everyone, everyone), jnp.bfloat16),
        scratch_shapes=[
            pltpu.VMEM((everyone, everyone), jnp.float32),
            pltpu.VMEM((everyone, everyone), jnp.float32),
            pltpu.VMEM((2, everyone // 2, everyone // 2), jnp.float32),
        ],
        compiler_params=pltpu.CompilerParams(vmem_limit_bytes=16 * MIB),
        cost_estimate=pl.CostEstimate(flops=1 << 30, bytes_accessed=30 * MIB, transcendentals=0),
        name="solve",
    )(whole)
    factor = 1.0 / math.sqrt(everyone - 1)
    changes = pl.pallas_call(
        functools.partial(shared_kernel, factor),
        out_shape=jax.ShapeDtypeStruct((everyone, cells), jnp.bfloat16),
        compiler_params=pltpu.CompilerParams(vmem_limit_bytes=50 * MIB),
        name="shared",
    )(mix, shared)
    changes = lax.all_to_all(changes.reshape(mems, members, cells), "mem", 0, 0)
    updated = finish(theta.reshape(members, lines_here, lanes), changes).reshape(theta.shape)
    return (updated, predicted)


def solution(mesh):
    in_specs = (
        P("mem", "space", None, None),
        P("space", None, None),
        P(),
        P("space"),
        P("space", "mem"),
        P("space"),
    )
    out_specs = (P("mem", "space", None, None), P("space", "mem"))
    return jax.shard_map(body, mesh=mesh, in_specs=in_specs, out_specs=out_specs, check_vma=False)
```

```python
import functools
import math

import jax
import jax.numpy as jnp
from jax import lax
from jax.experimental import pallas as pl
from jax.experimental.pallas import tpu as pltpu
from jax.sharding import PartitionSpec as P

STEPS = 3
STEP_SIZE = 0.055
OUTSIDE = 1.0 / (2.0 * STEP_SIZE)
HIGH = lax.Precision.HIGHEST
NT = (((1,), (1,)), ((), ()))
MIB = 1 << 20
PIVOTS = 8


def inverse(x):
    return pl.reciprocal(x, approx=True)


def diffuse_kernel(
    edge_ref, theta_ref, low_ref, high_ref, low_start_ref, high_start_ref, own_start_ref,
    out_ref, cx, cy, cz, keep, u0, u1, u2, u3,
):
    members, planes, rows, lanes = theta_ref.shape
    width = low_ref.shape[1]
    total = planes + 2 * width
    row_at = lax.broadcasted_iota(jnp.int32, (rows, lanes), 0)
    lane_at = lax.broadcasted_iota(jnp.int32, (rows, lanes), 1)
    last_row, last_lane = row_at == rows - 1, lane_at == lanes - 1
    sides = (
        (row_at == 0).astype(jnp.float32)
        + last_row.astype(jnp.float32)
        + (lane_at == 0).astype(jnp.float32)
        + last_lane.astype(jnp.float32)
    )
    low_edge, high_edge = edge_ref[0], edge_ref[1]

    @pl.when(pl.program_id(0) == 0)
    def _():
        u0[0:width] = low_start_ref[0].astype(jnp.float32) + low_start_ref[1].astype(jnp.float32)
        u0[width : width + planes] = own_start_ref[...]
        u0[width + planes :] = high_start_ref[0].astype(jnp.float32) + high_start_ref[1].astype(jnp.float32)

    def up(v, axis):
        return pltpu.roll(v, v.shape[axis] - 1, axis)

    def down(v, axis):
        return pltpu.roll(v, 1, axis)

    @pl.loop(0, members, unroll=2)
    def _(m):
        def resistance(p):
            if p < width:
                t = low_ref[m, p].astype(jnp.float32)
            elif p < width + planes:
                t = theta_ref[m, p - width]
            else:
                t = high_ref[m, p - width - planes].astype(jnp.float32)
            return jnp.exp(math.log(OUTSIDE) - t)

        fields = [u0, u1, u2, u3]
        flux_z = [None] * STEPS

        def advance(step, p):
            source = fields[step]
            u = source[p]
            if flux_z[step] is None:
                flux_z[step] = cz[p - 1] * (u - source[p - 1])
            fx = cx[p] * (up(u, 0) - u)
            fy = cy[p] * (up(u, 1) - u)
            fz = cz[p] * (source[p + 1] - u)
            new = keep[p] * u + ((fx - down(fx, 0)) + (fy - down(fy, 1)) + (fz - flux_z[step]))
            flux_z[step] = fz
            if p < width:
                new = new * low_edge
            elif p >= width + planes:
                new = new * high_edge
            if step == STEPS - 1:
                u3[p - width] = new
            else:
                fields[step + 1][p] = new

        before = None
        for p in range(total):
            r = resistance(p)
            if before is not None:
                cz[p - 1] = inverse(before + r)
            before = r
            if 1 <= p < total - 1:
                cx[p] = jnp.where(last_row, 0.0, inverse(r + up(r, 0)))
                cy[p] = jnp.where(last_lane, 0.0, inverse(r + up(r, 1)))
                keep[p] = 1.0 - sides * inverse(r + OUTSIDE)
            for step in range(STEPS):
                q = p - 1 - step
                if step + 1 <= q < total - 1 - step:
                    advance(step, q)
        ones = jnp.ones((8, lanes), jnp.float32)
        sums = lax.dot_general(
            ones, u3[...].reshape(planes * rows, lanes), NT, precision=HIGH, preferred_element_type=jnp.float32
        )
        out_ref[pl.ds(m, 1), :] = sums[0:1]


def diffuse(theta, first, low, high, begin_low, begin_high, start, edges):
    planes, rows, lanes = theta.shape[1:]
    members, width = low.shape[:2]
    members -= members % 8
    total = planes + 2 * width
    some = 8
    skip, last = first // some, begin_low.shape[0] // 2 - 1
    shape = (total, rows, lanes)
    return pl.pallas_call(
        diffuse_kernel,
        grid=(members // some,),
        in_specs=[
            pl.BlockSpec(memory_space=pltpu.SMEM),
            pl.BlockSpec((some, planes, rows, lanes), lambda i: (i + skip, 0, 0, 0)),
            pl.BlockSpec((some, width, rows, lanes), lambda i: (i, 0, 0, 0)),
            pl.BlockSpec((some, width, rows, lanes), lambda i: (i, 0, 0, 0)),
            pl.BlockSpec((2, width, rows, lanes), lambda i: (last, 0, 0, 0)),
            pl.BlockSpec((2, width, rows, lanes), lambda i: (last, 0, 0, 0)),
            pl.BlockSpec((planes, rows, lanes), lambda i: (0, 0, 0)),
        ],
        out_specs=pl.BlockSpec((some, planes * rows), lambda i: (i, 0)),
        out_shape=jax.ShapeDtypeStruct((members, planes * rows), jnp.float32),
        scratch_shapes=[pltpu.VMEM(shape, jnp.float32)] * 7 + [pltpu.VMEM((planes, rows, lanes), jnp.float32)],
        compiler_params=pltpu.CompilerParams(vmem_limit_bytes=50 * MIB),
        cost_estimate=pl.CostEstimate(flops=300 * theta.size, bytes_accessed=50 * theta.size, transcendentals=12 * theta.size),
        name="diffuse",
    )(edges, theta, low, high, begin_low, begin_high, start)


def gram_kernel(scale, lines_ref, data_ref, weight_ref, out_ref):
    everyone, count = lines_ref.shape
    value = lines_ref[...] * scale
    dev = value - jnp.mean(value, axis=0, keepdims=True)
    weight = weight_ref[0:1, :]
    dot = functools.partial(lax.dot_general, dimension_numbers=NT, precision=HIGH, preferred_element_type=jnp.float32)
    gram = dot(dev * (weight * (1.0 / (everyone - 1))), dev)
    right = dot((data_ref[...] - weight * value) * (1.0 / math.sqrt(everyone - 1)), dev)
    chunks = out_ref.shape[0]
    a = everyone // chunks
    for c in range(chunks):
        out_ref[c, 0:a] = gram[a * c : a * (c + 1)]
        out_ref[c, a:] = right[a * c : a * (c + 1)]


def invert_block(block):
    size = block.shape[0]
    lane_at = lax.broadcasted_iota(jnp.int32, (1, size), 1)
    row_at = lax.broadcasted_iota(jnp.int32, (8, 1), 0)
    groups = [block[8 * g : 8 * g + 8] for g in range(size // 8)]
    span = range(PIVOTS)
    for k in range(0, size, PIVOTS):
        g, s = divmod(k, 8)
        here = (lane_at >= k) & (lane_at < k + PIVOTS)
        rows = [groups[g][s + i : s + i + 1] for i in span]
        pivot = [[jnp.broadcast_to(row[:, k + j : k + j + 1], (1, size)) for j in span] for row in rows]
        rows = [jnp.where(here, (lane_at == k + i).astype(jnp.float32), row) for i, row in enumerate(rows)]
        for i in span:
            d = inverse(pivot[i][i])
            rows[i] = rows[i] * d
            for j in range(i + 1, PIVOTS):
                pivot[i][j] = pivot[i][j] * d
            for other in span:
                if other != i:
                    f = pivot[other][i]
                    rows[other] = rows[other] - f * rows[i]
                    for j in range(i + 1, PIVOTS):
                        pivot[other][j] = pivot[other][j] - f * pivot[i][j]
        new = []
        for i, old in enumerate(groups):
            next_rows = jnp.where(here, 0.0, old)
            for j in span:
                next_rows = next_rows - old[:, k + j : k + j + 1] * rows[j]
            if i == g:
                for j in span:
                    next_rows = jnp.where(row_at == s + j, rows[j], next_rows)
            new.append(next_rows)
        groups = new
    return jnp.concatenate(groups, axis=0)


def solve_kernel(parts_ref, out_ref, work, rhs, inv):
    chunks, depth, size = parts_ref.shape
    a = size // chunks
    half = size // 2
    for c in range(chunks):
        work[a * c : a * (c + 1)] = parts_ref[c, 0:a]
        rhs[a * c : a * (c + 1)] = parts_ref[c, a:]
    eye = (
        lax.broadcasted_iota(jnp.int32, (half, half), 0) == lax.broadcasted_iota(jnp.int32, (half, half), 1)
    ).astype(jnp.float32)
    work[0:half, 0:half] += eye
    work[half:, half:] += eye
    dot = functools.partial(jnp.dot, precision=HIGH, preferred_element_type=jnp.float32)

    @pl.loop(0, 2)
    def _(i):
        at = pl.ds(pl.multiple_of(i * half, half), half)

        @pl.when(i == 1)
        def _():
            cross = dot(work[half:, 0:half], inv[0])
            work[half:, half:] = work[half:, half:] - dot(cross, work[0:half, half:])

        inv[i] = invert_block(work[at, at])

    cross = dot(work[half:, 0:half], inv[0])
    first = dot(rhs[:, 0:half], inv[0])
    second = dot(rhs[:, half:] - dot(first, work[0:half, half:]), inv[1])
    out_ref[:, 0:half] = (first - dot(second, cross)).astype(jnp.bfloat16)
    out_ref[:, half:] = second.astype(jnp.bfloat16)


def shared_kernel(scale, mix_ref, fields_ref, out_ref):
    some = 512
    for c in range(0, out_ref.shape[1], some):
        result = jnp.dot(mix_ref[...], fields_ref[:, c : c + some], preferred_element_type=jnp.float32)
        out_ref[:, c : c + some] = (result * scale).astype(jnp.bfloat16)


def finish_kernel(theta_ref, change_ref, out_ref):
    members, _, lanes = theta_ref.shape
    chunks, _, cells = change_ref.shape
    some = cells // lanes
    for c in range(chunks):
        change = change_ref[c].astype(jnp.float32)
        rows = slice(c * some, (c + 1) * some)
        for m in range(0, members, 8):
            turned = jnp.stack([change[m : m + 8, r * lanes : (r + 1) * lanes] for r in range(some)])
            out_ref[m : m + 8, rows] = theta_ref[m : m + 8, rows] + jnp.swapaxes(turned, 0, 1)


def finish(theta, changes):
    members, rows, lanes = theta.shape
    chunks, _, cells = changes.shape
    block = pl.BlockSpec((members, rows // 2, lanes), lambda i: (0, i, 0))
    return pl.pallas_call(
        finish_kernel,
        grid=(2,),
        in_specs=[block, pl.BlockSpec((chunks // 2, members, cells), lambda i: (i, 0, 0))],
        out_specs=block,
        out_shape=jax.ShapeDtypeStruct(theta.shape, jnp.float32),
        compiler_params=pltpu.CompilerParams(vmem_limit_bytes=50 * MIB),
        cost_estimate=pl.CostEstimate(flops=2 * changes.size, bytes_accessed=10 * changes.size, transcendentals=0),
        name="finish",
    )(theta, changes)


def after(block, *others):
    return lax.optimization_barrier((block,) + others)[0]


def spread_out(block, axis):
    count = lax.axis_size(axis)
    return lax.all_to_all(jnp.broadcast_to(block[None], (count,) + block.shape), axis, 0, 0)


def after(block, *others):
    return lax.optimization_barrier((block,) + others)[0]


def body(theta, start, sensors, observed, noise, variance):
    members, planes, rows, lanes = theta.shape
    spaces, mems = lax.axis_size("space"), lax.axis_size("mem")
    lines_here = planes * rows
    everyone = members * mems
    mine, me = lax.axis_index("space"), lax.axis_index("mem")
    width = STEPS
    scale = 1.0 / math.sqrt(lanes)
    line_at = jnp.arange(spaces * lines_here, dtype=jnp.int32)
    rows_here = observed.shape[0]
    sensors_here = lax.dynamic_slice_in_dim(sensors, mine * rows_here, rows_here, 0)
    pick = (sensors_here[:, None] == line_at[None, :]).astype(jnp.float32)
    inv_var = 1.0 / variance
    data = jnp.concatenate([(observed[None, :] + noise.T) * inv_var[None, :], inv_var[None, :]], axis=0)
    data = jnp.pad(data, ((0, 7), (0, 0)))
    by_line = jnp.dot(data, pick, precision=HIGH).reshape(members + 8, spaces, lines_here).transpose(1, 0, 2)
    by_line = lax.all_to_all(by_line, "space", 0, 0)
    low_theta = theta.astype(jnp.bfloat16)
    coarse = lax.reduce_precision(start, 8, 7)
    fine = (start - coarse).astype(jnp.bfloat16)
    begin = jnp.stack([coarse.astype(jnp.bfloat16), fine])
    forward = [(i, i + 1) for i in range(spaces - 1)]
    backward = [(i + 1, i) for i in range(spaces - 1)]
    half = members // 2
    top, bottom = slice(planes - width, planes), slice(0, width)
    to_high = jnp.concatenate([low_theta[:half, top], begin[:, top]], axis=0)
    to_low = jnp.concatenate([low_theta[:half, bottom], begin[:, bottom]], axis=0)
    to_high_b, to_low_b = low_theta[half:, top], low_theta[half:, bottom]
    share_rows = lines_here // mems
    shares = low_theta.reshape(members, mems, share_rows, lanes).transpose(1, 0, 2, 3)
    shares = after(shares, by_line, to_high, to_low, to_high_b, to_low_b)
    halo_low = lax.ppermute(to_high, "space", forward)
    halo_high = lax.ppermute(to_low, "space", backward)
    halo_low_b = lax.ppermute(to_high_b, "space", forward)
    halo_high_b = lax.ppermute(to_low_b, "space", backward)
    edges = jnp.stack([mine > 0, mine < spaces - 1]).astype(jnp.float32)

    shared = lax.all_to_all(shares, "mem", 0, 0)
    cells = share_rows * lanes

    lines_a = diffuse(theta, 0, halo_low, halo_high, halo_low, halo_high, start, edges)
    lines_b = diffuse(theta, half, halo_low_b, halo_high_b, halo_low, halo_high, start, after(edges, lines_a))
    lines = jnp.concatenate([lines_a, lines_b], axis=0)
    lines, shared = lax.optimization_barrier((lines, shared))
    by_line = jnp.sum(by_line, axis=0)
    weights = by_line[members:]
    both = spread_out(jnp.stack([lines, by_line[:members]]), "mem")
    both, shared = lax.optimization_barrier((both, shared.reshape(everyone, cells)))
    lines_all = both[:, 0].reshape(everyone, lines_here)
    data_all = both[:, 1].reshape(everyone, lines_here)
    partial_sums = pl.pallas_call(
        functools.partial(gram_kernel, scale),
        out_shape=jax.ShapeDtypeStruct((spaces, 2 * everyone // spaces, everyone), jnp.float32),
        compiler_params=pltpu.CompilerParams(vmem_limit_bytes=50 * MIB),
        name="gram",
    )(lines_all, data_all, weights)
    sums = jnp.sum(lax.all_to_all(partial_sums, "space", 0, 0), axis=0)
    whole = spread_out(sums, "space")

    lines_slabs = spread_out(after(lines, whole), "space")
    lines_slabs = lines_slabs.transpose(1, 0, 2).reshape(members, spaces * lines_here)
    predicted = (jnp.dot(lines_slabs, pick.T, precision=HIGH) * scale).T

    mix = pl.pallas_call(
        solve_kernel,
        out_shape=jax.ShapeDtypeStruct((everyone, everyone), jnp.bfloat16),
        scratch_shapes=[
            pltpu.VMEM((everyone, everyone), jnp.float32),
            pltpu.VMEM((everyone, everyone), jnp.float32),
            pltpu.VMEM((2, everyone // 2, everyone // 2), jnp.float32),
        ],
        compiler_params=pltpu.CompilerParams(vmem_limit_bytes=16 * MIB),
        cost_estimate=pl.CostEstimate(flops=1 << 30, bytes_accessed=30 * MIB, transcendentals=0),
        name="solve",
    )(whole)
    factor = 1.0 / math.sqrt(everyone - 1)
    piece = cells // 2
    changes = pl.pallas_call(
        functools.partial(shared_kernel, factor),
        grid=(cells // piece,),
        in_specs=[
            pl.BlockSpec((everyone, everyone), lambda i: (0, 0)),
            pl.BlockSpec((everyone, piece), lambda i: (0, i)),
        ],
        out_specs=pl.BlockSpec((everyone, piece), lambda i: (0, i)),
        out_shape=jax.ShapeDtypeStruct((everyone, cells), jnp.bfloat16),
        compiler_params=pltpu.CompilerParams(vmem_limit_bytes=60 * MIB),
        name="shared",
    )(mix, shared)
    changes = lax.all_to_all(changes.reshape(mems, members, cells), "mem", 0, 0)
    updated = finish(theta.reshape(members, lines_here, lanes), changes).reshape(theta.shape)
    return (updated, predicted)


def solution(mesh):
    in_specs = (
        P("mem", "space", None, None),
        P("space", None, None),
        P(),
        P("space"),
        P("space", "mem"),
        P("space"),
    )
    out_specs = (P("mem", "space", None, None), P("space", "mem"))
    return jax.shard_map(body, mesh=mesh, in_specs=in_specs, out_specs=out_specs, check_vma=False)
```

```python
import functools
import math

import jax
import jax.numpy as jnp
from jax import lax
from jax.experimental import pallas as pl
from jax.experimental.pallas import tpu as pltpu
from jax.sharding import PartitionSpec as P

STEPS = 3
STEP_SIZE = 0.055
OUTSIDE = 1.0 / (2.0 * STEP_SIZE)
HIGH = lax.Precision.HIGHEST
NT = (((1,), (1,)), ((), ()))
MIB = 1 << 20
PIVOTS = 8


def inverse(x):
    return pl.reciprocal(x, approx=True)


def diffuse_kernel(
    edge_ref, theta_ref, low_ref, high_ref, low_start_ref, high_start_ref, own_start_ref,
    out_ref, cx, cy, cz, keep, u0, u1, u2, u3,
):
    members, planes, rows, lanes = theta_ref.shape
    width = low_ref.shape[1]
    total = planes + 2 * width
    row_at = lax.broadcasted_iota(jnp.int32, (rows, lanes), 0)
    lane_at = lax.broadcasted_iota(jnp.int32, (rows, lanes), 1)
    last_row, last_lane = row_at == rows - 1, lane_at == lanes - 1
    sides = (
        (row_at == 0).astype(jnp.float32)
        + last_row.astype(jnp.float32)
        + (lane_at == 0).astype(jnp.float32)
        + last_lane.astype(jnp.float32)
    )
    low_edge, high_edge = edge_ref[0], edge_ref[1]

    @pl.when(pl.program_id(0) == 0)
    def _():
        u0[0:width] = low_start_ref[0].astype(jnp.float32) + low_start_ref[1].astype(jnp.float32)
        u0[width : width + planes] = own_start_ref[...]
        u0[width + planes :] = high_start_ref[0].astype(jnp.float32) + high_start_ref[1].astype(jnp.float32)

    def up(v, axis):
        return pltpu.roll(v, v.shape[axis] - 1, axis)

    def down(v, axis):
        return pltpu.roll(v, 1, axis)

    @pl.loop(0, members, unroll=2)
    def _(m):
        def resistance(p):
            if p < width:
                t = low_ref[m, p].astype(jnp.float32)
            elif p < width + planes:
                t = theta_ref[m, p - width]
            else:
                t = high_ref[m, p - width - planes].astype(jnp.float32)
            return jnp.exp(math.log(OUTSIDE) - t)

        fields = [u0, u1, u2, u3]
        flux_z = [None] * STEPS

        def advance(step, p):
            source = fields[step]
            u = source[p]
            if flux_z[step] is None:
                flux_z[step] = cz[p - 1] * (u - source[p - 1])
            fx = cx[p] * (up(u, 0) - u)
            fy = cy[p] * (up(u, 1) - u)
            fz = cz[p] * (source[p + 1] - u)
            new = keep[p] * u + ((fx - down(fx, 0)) + (fy - down(fy, 1)) + (fz - flux_z[step]))
            flux_z[step] = fz
            if p < width:
                new = new * low_edge
            elif p >= width + planes:
                new = new * high_edge
            if step == STEPS - 1:
                u3[p - width] = new
            else:
                fields[step + 1][p] = new

        before = None
        for p in range(total):
            r = resistance(p)
            if before is not None:
                cz[p - 1] = inverse(before + r)
            before = r
            if 1 <= p < total - 1:
                cx[p] = jnp.where(last_row, 0.0, inverse(r + up(r, 0)))
                cy[p] = jnp.where(last_lane, 0.0, inverse(r + up(r, 1)))
                keep[p] = 1.0 - sides * inverse(r + OUTSIDE)
            for step in range(STEPS):
                q = p - 1 - step
                if step + 1 <= q < total - 1 - step:
                    advance(step, q)
        ones = jnp.ones((8, lanes), jnp.float32)
        sums = lax.dot_general(
            ones, u3[...].reshape(planes * rows, lanes), NT, precision=HIGH, preferred_element_type=jnp.float32
        )
        out_ref[pl.ds(m, 1), :] = sums[0:1]


def diffuse(theta, first, low, high, begin_low, begin_high, start, edges):
    planes, rows, lanes = theta.shape[1:]
    members, width = low.shape[:2]
    members -= members % 8
    total = planes + 2 * width
    some = 8
    skip, last = first // some, begin_low.shape[0] // 2 - 1
    shape = (total, rows, lanes)
    return pl.pallas_call(
        diffuse_kernel,
        grid=(members // some,),
        in_specs=[
            pl.BlockSpec(memory_space=pltpu.SMEM),
            pl.BlockSpec((some, planes, rows, lanes), lambda i: (i + skip, 0, 0, 0)),
            pl.BlockSpec((some, width, rows, lanes), lambda i: (i, 0, 0, 0)),
            pl.BlockSpec((some, width, rows, lanes), lambda i: (i, 0, 0, 0)),
            pl.BlockSpec((2, width, rows, lanes), lambda i: (last, 0, 0, 0)),
            pl.BlockSpec((2, width, rows, lanes), lambda i: (last, 0, 0, 0)),
            pl.BlockSpec((planes, rows, lanes), lambda i: (0, 0, 0)),
        ],
        out_specs=pl.BlockSpec((some, planes * rows), lambda i: (i, 0)),
        out_shape=jax.ShapeDtypeStruct((members, planes * rows), jnp.float32),
        scratch_shapes=[pltpu.VMEM(shape, jnp.float32)] * 7 + [pltpu.VMEM((planes, rows, lanes), jnp.float32)],
        compiler_params=pltpu.CompilerParams(vmem_limit_bytes=50 * MIB),
        cost_estimate=pl.CostEstimate(flops=300 * theta.size, bytes_accessed=50 * theta.size, transcendentals=12 * theta.size),
        name="diffuse",
    )(edges, theta, low, high, begin_low, begin_high, start)


def gram_kernel(scale, lines_ref, data_ref, weight_ref, out_ref):
    everyone, count = lines_ref.shape
    value = lines_ref[...] * scale
    dev = value - jnp.mean(value, axis=0, keepdims=True)
    weight = weight_ref[0:1, :]
    dot = functools.partial(lax.dot_general, dimension_numbers=NT, precision=HIGH, preferred_element_type=jnp.float32)
    gram = dot(dev * (weight * (1.0 / (everyone - 1))), dev)
    right = dot((data_ref[...] - weight * value) * (1.0 / math.sqrt(everyone - 1)), dev)
    chunks = out_ref.shape[0]
    a = everyone // chunks
    for c in range(chunks):
        out_ref[c, 0:a] = gram[a * c : a * (c + 1)]
        out_ref[c, a:] = right[a * c : a * (c + 1)]


def invert_block(block):
    size = block.shape[0]
    lane_at = lax.broadcasted_iota(jnp.int32, (1, size), 1)
    row_at = lax.broadcasted_iota(jnp.int32, (8, 1), 0)
    groups = [block[8 * g : 8 * g + 8] for g in range(size // 8)]
    span = range(PIVOTS)
    for k in range(0, size, PIVOTS):
        g, s = divmod(k, 8)
        here = (lane_at >= k) & (lane_at < k + PIVOTS)
        rows = [groups[g][s + i : s + i + 1] for i in span]
        pivot = [[jnp.broadcast_to(row[:, k + j : k + j + 1], (1, size)) for j in span] for row in rows]
        rows = [jnp.where(here, (lane_at == k + i).astype(jnp.float32), row) for i, row in enumerate(rows)]
        for i in span:
            d = inverse(pivot[i][i])
            rows[i] = rows[i] * d
            for j in range(i + 1, PIVOTS):
                pivot[i][j] = pivot[i][j] * d
            for other in span:
                if other != i:
                    f = pivot[other][i]
                    rows[other] = rows[other] - f * rows[i]
                    for j in range(i + 1, PIVOTS):
                        pivot[other][j] = pivot[other][j] - f * pivot[i][j]
        new = []
        for i, old in enumerate(groups):
            next_rows = jnp.where(here, 0.0, old)
            for j in span:
                next_rows = next_rows - old[:, k + j : k + j + 1] * rows[j]
            if i == g:
                for j in span:
                    next_rows = jnp.where(row_at == s + j, rows[j], next_rows)
            new.append(next_rows)
        groups = new
    return jnp.concatenate(groups, axis=0)


def solve_kernel(parts_ref, out_ref, work, rhs, inv):
    chunks, depth, size = parts_ref.shape
    a = size // chunks
    half = size // 2
    for c in range(chunks):
        work[a * c : a * (c + 1)] = parts_ref[c, 0:a]
        rhs[a * c : a * (c + 1)] = parts_ref[c, a:]
    eye = (
        lax.broadcasted_iota(jnp.int32, (half, half), 0) == lax.broadcasted_iota(jnp.int32, (half, half), 1)
    ).astype(jnp.float32)
    work[0:half, 0:half] += eye
    work[half:, half:] += eye
    dot = functools.partial(jnp.dot, precision=HIGH, preferred_element_type=jnp.float32)

    @pl.loop(0, 2)
    def _(i):
        at = pl.ds(pl.multiple_of(i * half, half), half)

        @pl.when(i == 1)
        def _():
            cross = dot(work[half:, 0:half], inv[0])
            work[half:, half:] = work[half:, half:] - dot(cross, work[0:half, half:])

        inv[i] = invert_block(work[at, at])

    cross = dot(work[half:, 0:half], inv[0])
    first = dot(rhs[:, 0:half], inv[0])
    second = dot(rhs[:, half:] - dot(first, work[0:half, half:]), inv[1])
    out_ref[:, 0:half] = (first - dot(second, cross)).astype(jnp.bfloat16)
    out_ref[:, half:] = second.astype(jnp.bfloat16)


def shared_kernel(scale, mix_ref, fields_ref, out_ref):
    some = 512
    for c in range(0, out_ref.shape[1], some):
        result = jnp.dot(mix_ref[...], fields_ref[:, c : c + some], preferred_element_type=jnp.float32)
        out_ref[:, c : c + some] = (result * scale).astype(jnp.bfloat16)


def finish_kernel(theta_ref, change_ref, out_ref):
    members, _, lanes = theta_ref.shape
    chunks, _, cells = change_ref.shape
    some = cells // lanes
    for c in range(chunks):
        change = change_ref[c].astype(jnp.float32)
        rows = slice(c * some, (c + 1) * some)
        for m in range(0, members, 8):
            turned = jnp.stack([change[m : m + 8, r * lanes : (r + 1) * lanes] for r in range(some)])
            out_ref[m : m + 8, rows] = theta_ref[m : m + 8, rows] + jnp.swapaxes(turned, 0, 1)


def finish(theta, changes):
    members, rows, lanes = theta.shape
    chunks, _, cells = changes.shape
    block = pl.BlockSpec((members, rows // 2, lanes), lambda i: (0, i, 0))
    return pl.pallas_call(
        finish_kernel,
        grid=(2,),
        in_specs=[block, pl.BlockSpec((chunks // 2, members, cells), lambda i: (i, 0, 0))],
        out_specs=block,
        out_shape=jax.ShapeDtypeStruct(theta.shape, jnp.float32),
        compiler_params=pltpu.CompilerParams(vmem_limit_bytes=50 * MIB),
        cost_estimate=pl.CostEstimate(flops=2 * changes.size, bytes_accessed=10 * changes.size, transcendentals=0),
        name="finish",
    )(theta, changes)


def after(block, *others):
    return lax.optimization_barrier((block,) + others)[0]


def spread_out(block, axis):
    count = lax.axis_size(axis)
    return lax.all_to_all(jnp.broadcast_to(block[None], (count,) + block.shape), axis, 0, 0)


def after(block, *others):
    return lax.optimization_barrier((block,) + others)[0]


def body(theta, start, sensors, observed, noise, variance):
    members, planes, rows, lanes = theta.shape
    spaces, mems = lax.axis_size("space"), lax.axis_size("mem")
    lines_here = planes * rows
    everyone = members * mems
    mine, me = lax.axis_index("space"), lax.axis_index("mem")
    width = STEPS
    scale = 1.0 / math.sqrt(lanes)
    line_at = jnp.arange(spaces * lines_here, dtype=jnp.int32)
    rows_here = observed.shape[0]
    sensors_here = lax.dynamic_slice_in_dim(sensors, mine * rows_here, rows_here, 0)
    pick = (sensors_here[:, None] == line_at[None, :]).astype(jnp.float32)
    inv_var = 1.0 / variance
    data = jnp.concatenate([(observed[None, :] + noise.T) * inv_var[None, :], inv_var[None, :]], axis=0)
    data = jnp.pad(data, ((0, 7), (0, 0)))
    by_line = jnp.dot(data, pick, precision=HIGH).reshape(members + 8, spaces, lines_here).transpose(1, 0, 2)
    by_line = lax.all_to_all(by_line, "space", 0, 0)
    low_theta = theta.astype(jnp.bfloat16)
    coarse = lax.reduce_precision(start, 8, 7)
    fine = (start - coarse).astype(jnp.bfloat16)
    begin = jnp.stack([coarse.astype(jnp.bfloat16), fine])
    forward = [(i, i + 1) for i in range(spaces - 1)]
    backward = [(i + 1, i) for i in range(spaces - 1)]
    half = members // 2
    top, bottom = slice(planes - width, planes), slice(0, width)
    to_high = jnp.concatenate([low_theta[:half, top], begin[:, top]], axis=0)
    to_low = jnp.concatenate([low_theta[:half, bottom], begin[:, bottom]], axis=0)
    to_high_b, to_low_b = low_theta[half:, top], low_theta[half:, bottom]
    share_rows = lines_here // mems
    shares = low_theta.reshape(members, mems, share_rows, lanes).transpose(1, 0, 2, 3)
    shares = after(shares, by_line, to_high, to_low, to_high_b, to_low_b)
    halo_low = lax.ppermute(to_high, "space", forward)
    halo_high = lax.ppermute(to_low, "space", backward)
    halo_low_b = lax.ppermute(to_high_b, "space", forward)
    halo_high_b = lax.ppermute(to_low_b, "space", backward)
    edges = jnp.stack([mine > 0, mine < spaces - 1]).astype(jnp.float32)

    shared = lax.all_to_all(shares, "mem", 0, 0)
    cells = share_rows * lanes

    lines_a = diffuse(theta, 0, halo_low, halo_high, halo_low, halo_high, start, edges)
    lines_b = diffuse(theta, half, halo_low_b, halo_high_b, halo_low, halo_high, start, after(edges, lines_a))
    lines = jnp.concatenate([lines_a, lines_b], axis=0)
    lines, shared = lax.optimization_barrier((lines, shared))
    by_line = jnp.sum(by_line, axis=0)
    weights = by_line[members:]
    both = spread_out(jnp.stack([lines, by_line[:members]]), "mem")
    both, shared = lax.optimization_barrier((both, shared.reshape(everyone, cells)))
    lines_all = both[:, 0].reshape(everyone, lines_here)
    data_all = both[:, 1].reshape(everyone, lines_here)
    partial_sums = pl.pallas_call(
        functools.partial(gram_kernel, scale),
        out_shape=jax.ShapeDtypeStruct((spaces, 2 * everyone // spaces, everyone), jnp.float32),
        compiler_params=pltpu.CompilerParams(vmem_limit_bytes=50 * MIB),
        name="gram",
    )(lines_all, data_all, weights)
    sums = jnp.sum(lax.all_to_all(partial_sums, "space", 0, 0), axis=0)
    whole = spread_out(sums, "space")

    lines_slabs = after(lines, whole)[None]
    owners = mine[None].astype(jnp.int32)
    early = None
    for k in (8, 4, 2, 1):
        other = lax.ppermute(lines_slabs, "space", [(i, i ^ k) for i in range(spaces)])
        early = other if k == 8 else early
        lines_slabs = jnp.concatenate([lines_slabs, other], axis=0)
        owners = jnp.concatenate([owners, owners ^ k])
    held = (owners[:, None] * lines_here + jnp.arange(lines_here, dtype=jnp.int32)[None, :]).reshape(-1)
    lines_slabs = lines_slabs.transpose(1, 0, 2).reshape(members, spaces * lines_here)
    picked = (held[:, None] == sensors_here[None, :]).astype(jnp.float32)
    predicted = (jnp.dot(lines_slabs, picked, precision=HIGH) * scale).T

    mix = pl.pallas_call(
        solve_kernel,
        out_shape=jax.ShapeDtypeStruct((everyone, everyone), jnp.bfloat16),
        scratch_shapes=[
            pltpu.VMEM((everyone, everyone), jnp.float32),
            pltpu.VMEM((everyone, everyone), jnp.float32),
            pltpu.VMEM((2, everyone // 2, everyone // 2), jnp.float32),
        ],
        compiler_params=pltpu.CompilerParams(vmem_limit_bytes=16 * MIB),
        cost_estimate=pl.CostEstimate(flops=1 << 30, bytes_accessed=30 * MIB, transcendentals=0),
        name="solve",
    )(whole)
    factor = 1.0 / math.sqrt(everyone - 1)
    mix = after(mix, early)
    piece = cells // 2
    changes = pl.pallas_call(
        functools.partial(shared_kernel, factor),
        grid=(cells // piece,),
        in_specs=[
            pl.BlockSpec((everyone, everyone), lambda i: (0, 0)),
            pl.BlockSpec((everyone, piece), lambda i: (0, i)),
        ],
        out_specs=pl.BlockSpec((everyone, piece), lambda i: (0, i)),
        out_shape=jax.ShapeDtypeStruct((everyone, cells), jnp.bfloat16),
        compiler_params=pltpu.CompilerParams(vmem_limit_bytes=60 * MIB),
        name="shared",
    )(mix, shared)
    changes = lax.all_to_all(changes.reshape(mems, members, cells), "mem", 0, 0)
    updated = finish(theta.reshape(members, lines_here, lanes), changes).reshape(theta.shape)
    return (updated, predicted)


def solution(mesh):
    in_specs = (
        P("mem", "space", None, None),
        P("space", None, None),
        P(),
        P("space"),
        P("space", "mem"),
        P("space"),
    )
    out_specs = (P("mem", "space", None, None), P("space", "mem"))
    return jax.shard_map(body, mesh=mesh, in_specs=in_specs, out_specs=out_specs, check_vma=False)
```

```python
import functools
import math

import jax
import jax.numpy as jnp
from jax import lax
from jax.experimental import pallas as pl
from jax.experimental.pallas import tpu as pltpu
from jax.sharding import PartitionSpec as P

STEPS = 3
STEP_SIZE = 0.055
OUTSIDE = 1.0 / (2.0 * STEP_SIZE)
HIGH = lax.Precision.HIGHEST
NT = (((1,), (1,)), ((), ()))
MIB = 1 << 20
PIVOTS = 8


def inverse(x):
    return pl.reciprocal(x, approx=True)


def diffuse_kernel(
    edge_ref, theta_ref, low_ref, high_ref, low_start_ref, high_start_ref, own_start_ref,
    out_ref, cx, cy, cz, keep, u0, u1, u2, u3,
):
    members, planes, rows, lanes = theta_ref.shape
    width = low_ref.shape[1]
    total = planes + 2 * width
    row_at = lax.broadcasted_iota(jnp.int32, (rows, lanes), 0)
    lane_at = lax.broadcasted_iota(jnp.int32, (rows, lanes), 1)
    last_row, last_lane = row_at == rows - 1, lane_at == lanes - 1
    sides = (
        (row_at == 0).astype(jnp.float32)
        + last_row.astype(jnp.float32)
        + (lane_at == 0).astype(jnp.float32)
        + last_lane.astype(jnp.float32)
    )
    low_edge, high_edge = edge_ref[0], edge_ref[1]

    @pl.when(pl.program_id(0) == 0)
    def _():
        u0[0:width] = low_start_ref[0].astype(jnp.float32) + low_start_ref[1].astype(jnp.float32)
        u0[width : width + planes] = own_start_ref[...]
        u0[width + planes :] = high_start_ref[0].astype(jnp.float32) + high_start_ref[1].astype(jnp.float32)

    def up(v, axis):
        return pltpu.roll(v, v.shape[axis] - 1, axis)

    def down(v, axis):
        return pltpu.roll(v, 1, axis)

    @pl.loop(0, members, unroll=2)
    def _(m):
        def resistance(p):
            if p < width:
                t = low_ref[m, p].astype(jnp.float32)
            elif p < width + planes:
                t = theta_ref[m, p - width]
            else:
                t = high_ref[m, p - width - planes].astype(jnp.float32)
            return jnp.exp(math.log(OUTSIDE) - t)

        fields = [u0, u1, u2, u3]
        flux_z = [None] * STEPS

        def advance(step, p):
            source = fields[step]
            u = source[p]
            if flux_z[step] is None:
                flux_z[step] = cz[p - 1] * (u - source[p - 1])
            fx = cx[p] * (up(u, 0) - u)
            fy = cy[p] * (up(u, 1) - u)
            fz = cz[p] * (source[p + 1] - u)
            new = keep[p] * u + ((fx - down(fx, 0)) + (fy - down(fy, 1)) + (fz - flux_z[step]))
            flux_z[step] = fz
            if p < width:
                new = new * low_edge
            elif p >= width + planes:
                new = new * high_edge
            if step == STEPS - 1:
                u3[p - width] = new
            else:
                fields[step + 1][p] = new

        before = None
        for p in range(total):
            r = resistance(p)
            if before is not None:
                cz[p - 1] = inverse(before + r)
            before = r
            if 1 <= p < total - 1:
                cx[p] = jnp.where(last_row, 0.0, inverse(r + up(r, 0)))
                cy[p] = jnp.where(last_lane, 0.0, inverse(r + up(r, 1)))
                keep[p] = 1.0 - sides * inverse(r + OUTSIDE)
            for step in range(STEPS):
                q = p - 1 - step
                if step + 1 <= q < total - 1 - step:
                    advance(step, q)
        ones = jnp.ones((8, lanes), jnp.float32)
        sums = lax.dot_general(
            ones, u3[...].reshape(planes * rows, lanes), NT, precision=HIGH, preferred_element_type=jnp.float32
        )
        out_ref[pl.ds(m, 1), :] = sums[0:1]


def diffuse(theta, first, low, high, begin_low, begin_high, start, edges):
    planes, rows, lanes = theta.shape[1:]
    members, width = low.shape[:2]
    members -= members % 8
    total = planes + 2 * width
    some = 8
    skip, last = first // some, begin_low.shape[0] // 2 - 1
    shape = (total, rows, lanes)
    return pl.pallas_call(
        diffuse_kernel,
        grid=(members // some,),
        in_specs=[
            pl.BlockSpec(memory_space=pltpu.SMEM),
            pl.BlockSpec((some, planes, rows, lanes), lambda i: (i + skip, 0, 0, 0)),
            pl.BlockSpec((some, width, rows, lanes), lambda i: (i, 0, 0, 0)),
            pl.BlockSpec((some, width, rows, lanes), lambda i: (i, 0, 0, 0)),
            pl.BlockSpec((2, width, rows, lanes), lambda i: (last, 0, 0, 0)),
            pl.BlockSpec((2, width, rows, lanes), lambda i: (last, 0, 0, 0)),
            pl.BlockSpec((planes, rows, lanes), lambda i: (0, 0, 0)),
        ],
        out_specs=pl.BlockSpec((some, planes * rows), lambda i: (i, 0)),
        out_shape=jax.ShapeDtypeStruct((members, planes * rows), jnp.float32),
        scratch_shapes=[pltpu.VMEM(shape, jnp.float32)] * 7 + [pltpu.VMEM((planes, rows, lanes), jnp.float32)],
        compiler_params=pltpu.CompilerParams(vmem_limit_bytes=50 * MIB),
        cost_estimate=pl.CostEstimate(flops=300 * theta.size, bytes_accessed=50 * theta.size, transcendentals=12 * theta.size),
        name="diffuse",
    )(edges, theta, low, high, begin_low, begin_high, start)


def gram_kernel(scale, lines_ref, data_ref, weight_ref, out_ref):
    everyone, count = lines_ref.shape
    value = lines_ref[...] * scale
    dev = value - jnp.mean(value, axis=0, keepdims=True)
    weight = weight_ref[0:1, :]
    dot = functools.partial(lax.dot_general, dimension_numbers=NT, precision=HIGH, preferred_element_type=jnp.float32)
    gram = dot(dev * (weight * (1.0 / (everyone - 1))), dev)
    right = dot((data_ref[...] - weight * value) * (1.0 / math.sqrt(everyone - 1)), dev)
    chunks = out_ref.shape[0]
    a = everyone // chunks
    for c in range(chunks):
        out_ref[c, 0:a] = gram[a * c : a * (c + 1)]
        out_ref[c, a:] = right[a * c : a * (c + 1)]


def invert_block(block):
    size = block.shape[0]
    lane_at = lax.broadcasted_iota(jnp.int32, (1, size), 1)
    row_at = lax.broadcasted_iota(jnp.int32, (8, 1), 0)
    groups = [block[8 * g : 8 * g + 8] for g in range(size // 8)]
    span = range(PIVOTS)
    for k in range(0, size, PIVOTS):
        g, s = divmod(k, 8)
        here = (lane_at >= k) & (lane_at < k + PIVOTS)
        rows = [groups[g][s + i : s + i + 1] for i in span]
        pivot = [[jnp.broadcast_to(row[:, k + j : k + j + 1], (1, size)) for j in span] for row in rows]
        rows = [jnp.where(here, (lane_at == k + i).astype(jnp.float32), row) for i, row in enumerate(rows)]
        for i in span:
            d = inverse(pivot[i][i])
            rows[i] = rows[i] * d
            for j in range(i + 1, PIVOTS):
                pivot[i][j] = pivot[i][j] * d
            for other in span:
                if other != i:
                    f = pivot[other][i]
                    rows[other] = rows[other] - f * rows[i]
                    for j in range(i + 1, PIVOTS):
                        pivot[other][j] = pivot[other][j] - f * pivot[i][j]
        new = []
        for i, old in enumerate(groups):
            next_rows = jnp.where(here, 0.0, old)
            for j in span:
                next_rows = next_rows - old[:, k + j : k + j + 1] * rows[j]
            if i == g:
                for j in span:
                    next_rows = jnp.where(row_at == s + j, rows[j], next_rows)
            new.append(next_rows)
        groups = new
    return jnp.concatenate(groups, axis=0)


def solve_kernel(parts_ref, out_ref, work, rhs, inv):
    chunks, depth, size = parts_ref.shape
    a = size // chunks
    half = size // 2
    for c in range(chunks):
        work[a * c : a * (c + 1)] = parts_ref[c, 0:a]
        rhs[a * c : a * (c + 1)] = parts_ref[c, a:]
    eye = (
        lax.broadcasted_iota(jnp.int32, (half, half), 0) == lax.broadcasted_iota(jnp.int32, (half, half), 1)
    ).astype(jnp.float32)
    work[0:half, 0:half] += eye
    work[half:, half:] += eye
    dot = functools.partial(jnp.dot, precision=HIGH, preferred_element_type=jnp.float32)

    @pl.loop(0, 2)
    def _(i):
        at = pl.ds(pl.multiple_of(i * half, half), half)

        @pl.when(i == 1)
        def _():
            cross = dot(work[half:, 0:half], inv[0])
            work[half:, half:] = work[half:, half:] - dot(cross, work[0:half, half:])

        inv[i] = invert_block(work[at, at])

    cross = dot(work[half:, 0:half], inv[0])
    first = dot(rhs[:, 0:half], inv[0])
    second = dot(rhs[:, half:] - dot(first, work[0:half, half:]), inv[1])
    out_ref[:, 0:half] = (first - dot(second, cross)).astype(jnp.bfloat16)
    out_ref[:, half:] = second.astype(jnp.bfloat16)


def shared_kernel(scale, mix_ref, fields_ref, out_ref):
    some = 512
    for c in range(0, out_ref.shape[1], some):
        result = jnp.dot(mix_ref[...], fields_ref[:, c : c + some], preferred_element_type=jnp.float32)
        out_ref[:, c : c + some] = (result * scale).astype(jnp.bfloat16)


def finish_kernel(theta_ref, change_ref, out_ref):
    members, _, lanes = theta_ref.shape
    chunks, _, cells = change_ref.shape
    some = cells // lanes
    for c in range(chunks):
        change = change_ref[c].astype(jnp.float32)
        rows = slice(c * some, (c + 1) * some)
        for m in range(0, members, 8):
            turned = jnp.stack([change[m : m + 8, r * lanes : (r + 1) * lanes] for r in range(some)])
            out_ref[m : m + 8, rows] = theta_ref[m : m + 8, rows] + jnp.swapaxes(turned, 0, 1)


def finish(theta, changes):
    members, rows, lanes = theta.shape
    chunks, _, cells = changes.shape
    block = pl.BlockSpec((members, rows // 2, lanes), lambda i: (0, i, 0))
    return pl.pallas_call(
        finish_kernel,
        grid=(2,),
        in_specs=[block, pl.BlockSpec((chunks // 2, members, cells), lambda i: (i, 0, 0))],
        out_specs=block,
        out_shape=jax.ShapeDtypeStruct(theta.shape, jnp.float32),
        compiler_params=pltpu.CompilerParams(vmem_limit_bytes=50 * MIB),
        cost_estimate=pl.CostEstimate(flops=2 * changes.size, bytes_accessed=10 * changes.size, transcendentals=0),
        name="finish",
    )(theta, changes)


def after(block, *others):
    return lax.optimization_barrier((block,) + others)[0]


def spread_out(block, axis):
    count = lax.axis_size(axis)
    return lax.all_to_all(jnp.broadcast_to(block[None], (count,) + block.shape), axis, 0, 0)


def after(block, *others):
    return lax.optimization_barrier((block,) + others)[0]


def body(theta, start, sensors, observed, noise, variance):
    members, planes, rows, lanes = theta.shape
    spaces, mems = lax.axis_size("space"), lax.axis_size("mem")
    lines_here = planes * rows
    everyone = members * mems
    mine, me = lax.axis_index("space"), lax.axis_index("mem")
    width = STEPS
    scale = 1.0 / math.sqrt(lanes)
    line_at = jnp.arange(spaces * lines_here, dtype=jnp.int32)
    rows_here = observed.shape[0]
    sensors_here = lax.dynamic_slice_in_dim(sensors, mine * rows_here, rows_here, 0)
    pick = (sensors_here[:, None] == line_at[None, :]).astype(jnp.float32)
    inv_var = 1.0 / variance
    data = jnp.concatenate([(observed[None, :] + noise.T) * inv_var[None, :], inv_var[None, :]], axis=0)
    data = jnp.pad(data, ((0, 7), (0, 0)))
    by_line = jnp.dot(data, pick, precision=HIGH).reshape(members + 8, spaces, lines_here).transpose(1, 0, 2)
    by_line = lax.all_to_all(by_line, "space", 0, 0)
    low_theta = theta.astype(jnp.bfloat16)
    coarse = lax.reduce_precision(start, 8, 7)
    fine = (start - coarse).astype(jnp.bfloat16)
    begin = jnp.stack([coarse.astype(jnp.bfloat16), fine])
    forward = [(i, i + 1) for i in range(spaces - 1)]
    backward = [(i + 1, i) for i in range(spaces - 1)]
    half = members // 4
    top, bottom = slice(planes - width, planes), slice(0, width)
    to_high = jnp.concatenate([low_theta[:half, top], begin[:, top]], axis=0)
    to_low = jnp.concatenate([low_theta[:half, bottom], begin[:, bottom]], axis=0)
    to_high_b, to_low_b = low_theta[half:, top], low_theta[half:, bottom]
    share_rows = lines_here // mems
    shares = low_theta.reshape(members, mems, share_rows, lanes).transpose(1, 0, 2, 3)
    shares = after(shares, by_line, to_high, to_low, to_high_b, to_low_b)
    halo_low = lax.ppermute(to_high, "space", forward)
    halo_high = lax.ppermute(to_low, "space", backward)
    halo_low_b = lax.ppermute(to_high_b, "space", forward)
    halo_high_b = lax.ppermute(to_low_b, "space", backward)
    edges = jnp.stack([mine > 0, mine < spaces - 1]).astype(jnp.float32)

    shared = lax.all_to_all(shares, "mem", 0, 0)
    cells = share_rows * lanes

    lines_a = diffuse(theta, 0, halo_low, halo_high, halo_low, halo_high, start, edges)
    lines_b = diffuse(theta, half, halo_low_b, halo_high_b, halo_low, halo_high, start, after(edges, lines_a))
    lines = jnp.concatenate([lines_a, lines_b], axis=0)
    lines, shared = lax.optimization_barrier((lines, shared))
    by_line = jnp.sum(by_line, axis=0)
    weights = by_line[members:]
    both = spread_out(jnp.stack([lines, by_line[:members]]), "mem")
    both, shared = lax.optimization_barrier((both, shared.reshape(everyone, cells)))
    lines_all = both[:, 0].reshape(everyone, lines_here)
    data_all = both[:, 1].reshape(everyone, lines_here)
    partial_sums = pl.pallas_call(
        functools.partial(gram_kernel, scale),
        out_shape=jax.ShapeDtypeStruct((spaces, 2 * everyone // spaces, everyone), jnp.float32),
        compiler_params=pltpu.CompilerParams(vmem_limit_bytes=50 * MIB),
        name="gram",
    )(lines_all, data_all, weights)
    sums = jnp.sum(lax.all_to_all(partial_sums, "space", 0, 0), axis=0)
    whole = spread_out(sums, "space")

    lines_slabs = after(lines, whole)[None]
    owners = mine[None].astype(jnp.int32)
    early = None
    for k in (8, 4, 2, 1):
        other = lax.ppermute(lines_slabs, "space", [(i, i ^ k) for i in range(spaces)])
        early = other if k == 8 else early
        lines_slabs = jnp.concatenate([lines_slabs, other], axis=0)
        owners = jnp.concatenate([owners, owners ^ k])
    held = (owners[:, None] * lines_here + jnp.arange(lines_here, dtype=jnp.int32)[None, :]).reshape(-1)
    lines_slabs = lines_slabs.transpose(1, 0, 2).reshape(members, spaces * lines_here)
    picked = (held[:, None] == sensors_here[None, :]).astype(jnp.float32)
    predicted = (jnp.dot(lines_slabs, picked, precision=HIGH) * scale).T

    mix = pl.pallas_call(
        solve_kernel,
        out_shape=jax.ShapeDtypeStruct((everyone, everyone), jnp.bfloat16),
        scratch_shapes=[
            pltpu.VMEM((everyone, everyone), jnp.float32),
            pltpu.VMEM((everyone, everyone), jnp.float32),
            pltpu.VMEM((2, everyone // 2, everyone // 2), jnp.float32),
        ],
        compiler_params=pltpu.CompilerParams(vmem_limit_bytes=16 * MIB),
        cost_estimate=pl.CostEstimate(flops=1 << 30, bytes_accessed=30 * MIB, transcendentals=0),
        name="solve",
    )(whole)
    factor = 1.0 / math.sqrt(everyone - 1)
    mix = after(mix, early)
    piece = cells // 2
    changes = pl.pallas_call(
        functools.partial(shared_kernel, factor),
        grid=(cells // piece,),
        in_specs=[
            pl.BlockSpec((everyone, everyone), lambda i: (0, 0)),
            pl.BlockSpec((everyone, piece), lambda i: (0, i)),
        ],
        out_specs=pl.BlockSpec((everyone, piece), lambda i: (0, i)),
        out_shape=jax.ShapeDtypeStruct((everyone, cells), jnp.bfloat16),
        compiler_params=pltpu.CompilerParams(vmem_limit_bytes=60 * MIB),
        name="shared",
    )(mix, shared)
    changes = lax.all_to_all(changes.reshape(mems, members, cells), "mem", 0, 0)
    updated = finish(theta.reshape(members, lines_here, lanes), changes).reshape(theta.shape)
    return (updated, predicted)


def solution(mesh):
    in_specs = (
        P("mem", "space", None, None),
        P("space", None, None),
        P(),
        P("space"),
        P("space", "mem"),
        P("space"),
    )
    out_specs = (P("mem", "space", None, None), P("space", "mem"))
    return jax.shard_map(body, mesh=mesh, in_specs=in_specs, out_specs=out_specs, check_vma=False)
```
